32 devices in a mesh: groups: 2 (over y), replica: 1, da: 4 (over x, core), db: 4 (over z).
Axes of the slice: x: 2, y: 2, z: 4, core: 2. Of those that a mesh axis runs over, the one named last changes fastest.
Arguments:
- tokens: bfloat16 [4096, 1024], P(('groups', 'replica', 'da', 'db')), parts along dimension 0, may hold values from -6 to 6
- grad_out: bfloat16 [4096, 1024], P(('groups', 'replica', 'da', 'db')), parts along dimension 0, may hold values from -3 to 3
- routes: int32 [4096, 8], P(('groups', 'replica', 'da', 'db')), parts along dimension 0, may hold values from 0 to 15, as said below
- gates: bfloat16 [4096, 8], P(('groups', 'replica', 'da', 'db')), parts along dimension 0, may hold values from 0.019897461 to 0.5
- w_gate_up: bfloat16 [16, 1024, 768], P(('da', 'db'), 'replica'), may hold values from -0.1875 to 0.1875
- w_down: bfloat16 [16, 384, 1024], P(('da', 'db'), 'replica'), may hold values from -0.3125 to 0.3125
Outputs:
- token_grads: bfloat16 [4096, 1024], P(('groups', 'replica', 'da', 'db')), parts along dimension 0
- gate_grads: bfloat16 [4096, 8], P(('groups', 'replica', 'da', 'db')), parts along dimension 0
- gate_up_grads: bfloat16 [32, 1024, 768], P(('groups', 'da', 'db'), 'replica'), parts along dimension 0
- down_grads: bfloat16 [32, 384, 1024], P(('groups', 'da', 'db'), 'replica'), parts along dimension 0
The draws below stay inside these ranges and needn't reach their ends.
There are 2 independent parts, one for each index of `groups`. The reference program is written for one: setup_inputs(seed, part) draws one part's arguments, and reference() takes and returns one part's arrays. A program takes and returns all parts, laid end to end along the dimension named above; an argument that names none is the same for every part. Nothing has to cross between parts.
Inputs may be any that keep to these rules, and one draw needn't show every extreme that they name: `routes`: each token names 8 different experts. In every aligned block of 2 consecutive tokens, each expert is named exactly once, so the tokens of one device name every expert exactly 64 times.
All inputs are finite; a program needn't handle non-finite values.
Results may differ from the reference program's by a relative error of at most 0.0085.
Values may be sent and summed in bfloat16 or wider, within the bound.
No kernel may reach another device: no remote copies, remote signals or barrier semaphores. Data moves between devices by JAX's collectives and lax.ppermute only.
A program may use at most 64 MiB of HBM per device.

```python
import math
import jax
import jax.numpy as jnp
from jax import lax

D = 1024
FF = 384
TOP = 8
TOK_DEV = 128
EXPERTS = 16
TOKENS = 2048
N_REPLICA = 1
N_DA = 4
N_DB = 4


def draw_routes(key, part):
    per_round = EXPERTS // TOP
    round_count = TOKENS // per_round
    keys = jax.random.split(jax.random.fold_in(key, 7), round_count)
    orders = jax.vmap(lambda one: jax.random.permutation(one, EXPERTS))(keys)
    return orders.reshape(TOKENS, TOP).astype(jnp.int32)


def block_levels(stream_key, shape, shards, least, top_value):
    def one(dim, shards_of):
        heights = jax.random.uniform(jax.random.fold_in(jax.random.fold_in(stream_key, 6), dim), (shards_of,), jnp.float32, least / len(shards), top_value / len(shards))
        return jnp.repeat(jnp.exp(heights), shape[dim] // shards_of).reshape((-1,) + (1,) * (len(shape) - dim - 1))

    loudness = one(*shards[0])
    for cut in shards[1:]:
        loudness = loudness * one(*cut)
    return loudness


def centred(own_key, extent, spread, most, cuts=(), held_as=jnp.bfloat16):
    array = jax.random.normal(own_key, extent, jnp.float32) * spread
    if len(cuts) > 0:
        array = block_levels(own_key, extent, cuts, -0.22, 0.18) * array
    return jnp.clip(array, min=-most, max=most).astype(held_as)


def setup_inputs(seed: int = 0, part: int = 0) -> dict:
    splits = jax.random.split(jax.random.key(seed), 7)
    own_keys = jax.random.split(jax.random.fold_in(splits[6], part), 7)
    return {
        "tokens": centred(own_keys[0], (TOKENS, D), 1.0, 6.0, ((0, 16),)),
        "grad_out": centred(own_keys[1], (TOKENS, D), 0.5, 3.0, ((0, 16),)),
        "routes": draw_routes(jax.random.fold_in(jax.random.fold_in(splits[6], part), 71), part),
        "gates": jnp.clip(jnp.exp(math.log(0.5) - 3.224016 * jax.random.uniform(own_keys[3], (TOKENS, TOP), jnp.float32) ** block_levels(own_keys[3], (TOKENS, TOP), ((0, 16),), -0.2, 0.2)), 0.019897461, 0.5).astype(jnp.bfloat16),
        "w_gate_up": centred(splits[4], (EXPERTS, D, 2 * FF), D ** -0.5, 0.1875, ((0, 16),)),
        "w_down": centred(splits[5], (EXPERTS, FF, D), FF ** -0.5, 0.3125, ((0, 16),)),
    }


def silu_parts(projected):
    sigmoid = jax.nn.sigmoid(projected)
    return projected * sigmoid, sigmoid * (1.0 + projected * (1.0 - sigmoid))


def replica_sum(partials):
    rounded = lax.optimization_barrier(partials.astype(jnp.bfloat16))
    return jnp.sum(rounded.astype(jnp.float32), axis=0).astype(jnp.bfloat16)


def reference(tokens, grad_out, routes, gates, w_gate_up, w_down):
    per_replica = TOK_DEV * N_DA * N_DB
    flat_routes = routes.reshape(N_REPLICA, per_replica * TOP)
    ordering = jnp.argsort(flat_routes, axis=1, stable=True).astype(jnp.int32)
    rows_expert = per_replica * TOP // EXPERTS
    ordering = ordering.reshape(N_REPLICA, EXPERTS, rows_expert)
    offsets = (jnp.arange(N_REPLICA, dtype=jnp.int32) * (per_replica * TOP)).astype(jnp.int32)
    route_index = (ordering + offsets[:, None, None]).astype(jnp.int32)
    route_index = jnp.transpose(route_index, (1, 0, 2))
    flat_gates = gates.reshape(-1)

    def expert_step(carry, inputs):
        token_acc, gate_acc = carry
        index, w_in, w_out = inputs
        token_ids = (index // TOP).astype(jnp.int32)
        input_rows = tokens[token_ids].astype(jnp.float32)
        upstream = grad_out[token_ids].astype(jnp.float32)
        gate_rows = flat_gates[index].astype(jnp.float32)[..., None]
        w_in_f = w_in.astype(jnp.float32)
        w_out_f = w_out.astype(jnp.float32)
        projected = jnp.einsum("prd,df->prf", input_rows, w_in_f)
        gate_part = projected[..., :FF]
        up_part = projected[..., FF:]
        activated, derivative = silu_parts(gate_part)
        hidden = (activated * up_part).astype(jnp.bfloat16)
        back_raw = jnp.einsum("prd,fd->prf", upstream, w_out_f)
        gate_scores = jnp.sum(hidden.astype(jnp.float32) * back_raw, axis=-1).astype(jnp.bfloat16)
        back_hidden = gate_rows * back_raw
        grad_projected = jnp.concatenate([back_hidden * up_part * derivative, back_hidden * activated], axis=-1).astype(jnp.bfloat16)
        scaled_upstream = (gate_rows * upstream).astype(jnp.bfloat16)
        input_grads = jnp.einsum("prf,df->prd", grad_projected.astype(jnp.float32), w_in_f).astype(jnp.bfloat16)
        grad_in = replica_sum(jnp.einsum("prd,prf->pdf", input_rows, grad_projected.astype(jnp.float32)))
        grad_down = replica_sum(jnp.einsum("prf,prd->pfd", hidden.astype(jnp.float32), scaled_upstream.astype(jnp.float32)))
        token_acc = token_acc.at[token_ids.reshape(-1)].add(input_grads.reshape(-1, D).astype(jnp.float32))
        gate_acc = gate_acc.at[index.reshape(-1)].set(gate_scores.reshape(-1))
        return (token_acc, gate_acc), (grad_in, grad_down)

    start = (jnp.zeros((TOKENS, D), jnp.float32), jnp.zeros((TOKENS * TOP,), jnp.bfloat16))
    (token_acc, gate_acc), (gate_up_grads, down_grads) = lax.scan(expert_step, start, (route_index, w_gate_up, w_down))
    return token_acc.astype(jnp.bfloat16), gate_acc.reshape(TOKENS, TOP), gate_up_grads, down_grads
```

```python
import functools

import jax
import jax.numpy as jnp
from jax import lax
from jax.experimental import pallas as pl
from jax.experimental.pallas import tpu as pltpu
from jax.sharding import PartitionSpec as P

LANES = 128
ROWS = 16
AXES = ("da", "db")
VMEM_LIMIT = 40 * 1024 * 1024


def silu_parts(projected):
    sigmoid = jax.nn.sigmoid(projected)
    return (projected * sigmoid, sigmoid * (1.0 + projected * (1.0 - sigmoid)))


def body(tokens, grad_out, routes, gates, w_gate_up, w_down):
    local_tokens, features = tokens.shape
    top_count = routes.shape[1]
    hidden_units = w_gate_up.shape[2] // 2
    first_size = lax.axis_size("da")
    second_size = lax.axis_size("db")
    experts = first_size * second_size
    per_round = experts // top_count
    rounds = local_tokens // per_round
    expert_ids = lax.broadcasted_iota(jnp.int32, (1, 1, 1, experts), 3)
    matches = routes.reshape(rounds, per_round, top_count, 1) == expert_ids
    gate_values = gates.reshape(rounds, per_round, top_count, 1).astype(jnp.float32)
    gate_table = jnp.sum(jnp.where(matches, gate_values, 0.0), axis=(1, 2)).astype(jnp.bfloat16)
    chosen = jnp.any(matches, axis=2).astype(jnp.bfloat16)
    input_send = jnp.einsum(
        "rge,rgd->red",
        chosen,
        tokens.reshape(rounds, per_round, features),
        preferred_element_type=jnp.float32,
    ).astype(jnp.bfloat16)
    upstream_send = jnp.einsum(
        "rge,rgd->red",
        chosen,
        grad_out.reshape(rounds, per_round, features),
        preferred_element_type=jnp.float32,
    ).astype(jnp.bfloat16)
    input_recv, upstream_recv, gate_recv = (
        lax.all_to_all(input_send, ("da", "db"), split_axis=1, concat_axis=1, tiled=True),
        lax.all_to_all(upstream_send, ("da", "db"), split_axis=1, concat_axis=1, tiled=True),
        lax.all_to_all(gate_table, ("da", "db"), split_axis=1, concat_axis=1, tiled=True),
    )
    input_rows = input_recv.reshape(-1, features)
    upstream_rows = upstream_recv.reshape(-1, features)
    gate_rows = gate_recv.reshape(-1, 1).astype(jnp.float32)
    w_in, w_out = (
        lax.all_gather(w_gate_up[0], "replica", axis=0, tiled=True),
        lax.all_gather(w_down[0], "replica", axis=0, tiled=True),
    )
    projected = jnp.dot(input_rows, w_in, preferred_element_type=jnp.float32)
    back_raw = jnp.einsum("rd,fd->rf", upstream_rows, w_out, preferred_element_type=jnp.float32)
    gate_part = projected[:, :hidden_units]
    up_part = projected[:, hidden_units:]
    activated, derivative = silu_parts(gate_part)
    hidden = (activated * up_part).astype(jnp.bfloat16)
    gate_scores = jnp.sum(hidden.astype(jnp.float32) * back_raw, axis=1).astype(jnp.bfloat16)
    back_hidden = gate_rows * back_raw
    grad_projected = jnp.concatenate(
        [back_hidden * up_part * derivative, back_hidden * activated], axis=1
    ).astype(jnp.bfloat16)
    scaled_upstream = (gate_rows * upstream_rows.astype(jnp.float32)).astype(jnp.bfloat16)
    input_grads = jnp.einsum("rf,df->rd", grad_projected, w_in, preferred_element_type=jnp.float32)
    input_grads = input_grads.astype(jnp.bfloat16).reshape(rounds, experts, features)
    score_back = gate_scores.reshape(rounds, experts)
    returned, score_ret = (
        lax.all_to_all(input_grads, ("da", "db"), split_axis=1, concat_axis=1, tiled=True),
        lax.all_to_all(score_back, ("da", "db"), split_axis=1, concat_axis=1, tiled=True),
    )
    score_ret = score_ret.reshape(rounds, 1, 1, experts).astype(jnp.float32)
    token_grads = (
        jnp.einsum("rge,red->rgd", chosen, returned, preferred_element_type=jnp.float32)
        .astype(jnp.bfloat16)
        .reshape(local_tokens, features)
    )
    gate_grads = (
        jnp.sum(jnp.where(matches, score_ret, 0.0), axis=3)
        .astype(jnp.bfloat16)
        .reshape(local_tokens, top_count)
    )
    columns = input_rows
    grad_in = lax.psum_scatter(
        jnp.einsum("rd,rf->df", columns, grad_projected, preferred_element_type=jnp.float32).astype(
            jnp.bfloat16
        ),
        "replica",
        scatter_dimension=0,
        tiled=True,
    )
    columns = hidden
    grad_down = lax.psum_scatter(
        jnp.einsum(
            "rf,rd->fd", columns, scaled_upstream, preferred_element_type=jnp.float32
        ).astype(jnp.bfloat16),
        "replica",
        scatter_dimension=0,
        tiled=True,
    )
    return (token_grads, gate_grads, grad_in[None], grad_down[None])


def dot(a, b, contract):
    return lax.dot_general(a, b, ((contract[:1], contract[1:]), ((), ())), preferred_element_type=jnp.float32)


def one_hot(table, expert, rounds, per_round):
    experts, count = table.shape
    rows = lax.broadcasted_iota(jnp.int32, (experts, count), 0)
    line = jnp.sum(jnp.where(rows == expert, table.astype(jnp.float32), 0.0), axis=0, keepdims=True)
    token_block = lax.broadcasted_iota(jnp.int32, (rounds, count), 1) // per_round
    mine = lax.broadcasted_iota(jnp.int32, (rounds, count), 0) == token_block
    return jnp.where(mine, line, 0.0)


def picks(table, ids, rounds, per_round):
    own = one_hot(table, ids[0], rounds, per_round)
    other = one_hot(table, ids[1], rounds, per_round)
    weights = jnp.concatenate([own, other], axis=0)
    return weights, jnp.where(weights != 0.0, 1.0, 0.0).astype(jnp.bfloat16)


def select_kernel(count, rounds, per_round, ids_ref, *refs):
    shards, (own_ref, other_ref) = refs[: 2 * count], refs[2 * count :]
    for j in range(count):
        token_ref, grad_ref = shards[2 * j], shards[2 * j + 1]
        local, features = grad_ref.shape
        table = token_ref[local:, :local]
        weights, chosen = picks(table, ids_ref, rounds, per_round)
        gate = jnp.sum(weights, axis=1, keepdims=True).astype(jnp.bfloat16)
        gate = jnp.broadcast_to(gate, (2 * rounds, LANES))
        left = dot(chosen, token_ref[:local, :], (1, 0)).astype(jnp.bfloat16)
        right = dot(chosen, grad_ref[...], (1, 0)).astype(jnp.bfloat16)
        for k, out in ((0, own_ref), (1, other_ref)):
            lines = slice(j * rounds, (j + 1) * rounds)
            half = slice(k * rounds, (k + 1) * rounds)
            out[lines, :features] = left[half]
            out[lines, features : 2 * features] = right[half]
            out[lines, 2 * features :] = gate[half]


def expert_kernel(ids_ref, own_ref, other_ref, w_in_ref, w_out_ref, grad_own, grad_other, x_ref, hid_ref, proj_ref, up_ref):
    features, double = w_in_ref.shape
    hidden_units = double // 2
    rows = own_ref.shape[0]
    w_in, w_out = w_in_ref[...], w_out_ref[...]
    for start, ref, out in ((0, own_ref, grad_own), (rows, other_ref, grad_other)):
        lines = slice(start, start + rows)
        x = ref[:, :features]
        upstream = ref[:, features : 2 * features]
        gate = ref[:, 2 * features : 2 * features + 1].astype(jnp.float32)
        projected = dot(x, w_in, (1, 0))
        back_raw = dot(upstream, w_out, (1, 1))
        gate_part, up_part = projected[:, :hidden_units], projected[:, hidden_units:]
        activated, derivative = silu_parts(gate_part)
        hidden = (activated * up_part).astype(jnp.bfloat16)
        score = jnp.sum(hidden.astype(jnp.float32) * back_raw, axis=1, keepdims=True)
        back_hidden = gate * back_raw
        grad_projected = jnp.concatenate(
            [back_hidden * up_part * derivative, back_hidden * activated], axis=1
        ).astype(jnp.bfloat16)
        x_ref[lines, :] = x
        hid_ref[lines, :] = hidden
        proj_ref[lines, :] = grad_projected
        up_ref[lines, :] = (gate * upstream.astype(jnp.float32)).astype(jnp.bfloat16)
        out[:, :features] = dot(grad_projected, w_in, (1, 1)).astype(jnp.bfloat16)
        lane = lax.broadcasted_iota(jnp.int32, (rows, LANES), 1)
        out[:, features:] = jnp.where(lane == ids_ref[0], score, 0.0).astype(jnp.bfloat16)


def spread_kernel(count, rounds, per_round, ids_ref, own_ref, other_ref, *refs):
    tables, outs = refs[:count], refs[count:]
    for j in range(count):
        local = outs[j].shape[0]
        _, chosen = picks(tables[j][:, :local], ids_ref, rounds, per_round)
        lines = slice(j * rounds, (j + 1) * rounds)
        grads = jnp.concatenate([own_ref[lines, :], other_ref[lines, :]], axis=0)
        outs[j][...] = dot(chosen, grads, (0, 0)).astype(jnp.bfloat16)


def weights_kernel(groups, *refs):
    ins, (grad_in_ref, grad_down_ref) = refs[: 4 * groups], refs[4 * groups :]
    for out, left, right in ((grad_in_ref, 0, 2), (grad_down_ref, 1, 3)):
        total = None
        for g in range(groups):
            part = dot(ins[4 * g + left][...], ins[4 * g + right][...], (0, 0))
            total = part if total is None else total + part
        out[0] = total.astype(jnp.bfloat16)


def call(kernel, outs, args, smem=1, cost=None, specs=None):
    in_specs = [pl.BlockSpec(memory_space=pltpu.SMEM)] * smem
    in_specs += specs or [pl.BlockSpec(memory_space=pltpu.VMEM)] * (len(args) - smem)
    return pl.pallas_call(
        kernel,
        out_shape=[jax.ShapeDtypeStruct(s, jnp.bfloat16) for s in outs],
        grid=(1,) if specs else (),
        in_specs=in_specs,
        out_specs=[pl.BlockSpec(memory_space=pltpu.VMEM)] * len(outs),
        compiler_params=pltpu.CompilerParams(vmem_limit_bytes=VMEM_LIMIT),
        cost_estimate=cost,
    )(*args)


def ring_body(sizes, tokens, grad_out, routes, gates, w_gate_up, w_down):
    first_size, second_size = sizes
    columns = first_size // 2
    local, features = tokens.shape
    top_count = routes.shape[1]
    experts = first_size * second_size
    per_round = experts // top_count
    rounds = local // per_round
    hidden_units = w_gate_up.shape[2] // 2
    ring = [(0, z) for z in range(second_size)] + [(1, z) for z in reversed(range(second_size))]
    length = len(ring)

    def device(place, core):
        x, z = ring[place % length]
        return (x * 2 + core) * second_size + z

    def shift(value, step):
        pairs = [(device(p, c), device(p + step, c)) for p in range(length) for c in range(2)]
        return lax.ppermute(value, AXES, pairs)

    def swap(value):
        pairs = [(device(p, c), device(p, 1 - c)) for p in range(length) for c in range(2)]
        return lax.ppermute(value, AXES, pairs)

    me, row = lax.axis_index("da"), lax.axis_index("db")
    core = lax.rem(me, 2)
    ids = jnp.stack([me * second_size + row, (me + 1 - 2 * core) * second_size + row]).astype(jnp.int32)

    expert_ids = lax.broadcasted_iota(jnp.int32, (experts, local, top_count), 0)
    matches = routes[None] == expert_ids
    table = jnp.sum(jnp.where(matches, gates[None].astype(jnp.float32), 0.0), axis=2).astype(jnp.bfloat16)
    table = jnp.pad(table, ((0, 0), (0, features - local)))
    first = jnp.concatenate([tokens, table], axis=0)

    half = length // 2
    shards = {0: (first, grad_out)}
    right, left = (first, grad_out), (first, grad_out)
    for step in range(1, half):
        right = (shift(right[0], 1), shift(right[1], 1))
        left = (shift(left[0], -1), shift(left[1], -1))
        shards[-step], shards[step] = right, left
    shards[half] = (shift(right[0], 1), shift(left[1], -1))

    w_in, w_out = w_gate_up[0], w_down[0]
    near = [0] + [s * k for k in range(1, half - 1) for s in (-1, 1)]
    far = [1 - half, half - 1, half]
    saved, sums = [], {}
    wide = 2 * features + LANES
    for group in (near, far):
        count = len(group)
        size = count * rounds
        own, other = call(
            functools.partial(select_kernel, count, rounds, per_round),
            [(size, wide)] * 2,
            [ids] + [a for k in group for a in shards[k]],
        )
        other = swap(other)
        own_grad, other_grad, *kept = call(
            expert_kernel,
            [(size, features + LANES)] * 2
            + [(2 * size, n) for n in (features, hidden_units, 2 * hidden_units, features)],
            [ids, own, other, w_in, w_out],
        )
        saved += kept
        other_grad = swap(other_grad)
        table_spec = pl.BlockSpec((experts, LANES * pl.cdiv(local, LANES)), lambda i: (local // experts, 0))
        spread = call(
            functools.partial(spread_kernel, count, rounds, per_round),
            [(local, features + LANES)] * count,
            [ids, own_grad, other_grad] + [shards[k][0] for k in group],
            specs=[pl.BlockSpec(memory_space=pltpu.VMEM)] * 2 + [table_spec] * count,
        )
        sums.update(zip(group, spread))

    grad_in, grad_down = call(
        functools.partial(weights_kernel, len(saved) // 4),
        [(1, features, 2 * hidden_units), (1, hidden_units, features)],
        saved,
        smem=0,
    )

    def add(*terms):
        return sum(t.astype(jnp.float32) for t in terms).astype(jnp.bfloat16)

    cut = features // 2
    right, left = shift(sums[half][:, :cut], 1), shift(sums[half][:, cut:], -1)
    to_right, to_left = sums[half - 1], sums[1 - half]
    right = jnp.concatenate([add(right, to_right[:, :cut]), to_right[:, cut:]], axis=1)
    left = jnp.concatenate([to_left[:, :cut], add(left, to_left[:, cut:])], axis=1)
    for k in range(half - 1, 0, -1):
        right, left = shift(right, 1), shift(left, -1)
        if k > 1:
            right, left = add(right, sums[k - 1]), add(left, sums[1 - k])
    total = add(right, left, sums[0])
    scores = total[:, features : features + experts]
    here = routes[:, :, None] == lax.broadcasted_iota(jnp.int32, (1, 1, experts), 2)
    gate_grads = jnp.sum(jnp.where(here, scores[:, None, :].astype(jnp.float32), 0.0), axis=2).astype(jnp.bfloat16)
    return total[:, :features], gate_grads, grad_in, grad_down


def solution(mesh):
    placed = (
        P(("groups", "replica", "da", "db"), None),
        P(("groups", "replica", "da", "db"), None),
        P(("groups", "replica", "da", "db"), None),
        P(("groups", "replica", "da", "db"), None),
        P(("da", "db"), "replica", None),
        P(("da", "db"), "replica", None),
    )
    first_size, second_size = mesh.shape["da"], mesh.shape["db"]
    experts = first_size * second_size

    def chosen_body(tokens, grad_out, routes, gates, w_gate_up, w_down):
        local, top_count = routes.shape
        dense = experts // top_count <= 2
        closed = mesh.shape["replica"] == 1 and first_size == 4 and second_size >= 2
        fits = local % LANES == 0 and local <= tokens.shape[1] and experts % ROWS == 0 and local % experts == 0
        fits = fits and experts <= LANES and (local * top_count // experts) % ROWS == 0
        args = (tokens, grad_out, routes, gates, w_gate_up, w_down)
        if dense and closed and fits:
            return ring_body((first_size, second_size), *args)
        return body(*args)

    return jax.shard_map(
        chosen_body,
        mesh=mesh,
        in_specs=placed,
        out_specs=(
            P(("groups", "replica", "da", "db"), None),
            P(("groups", "replica", "da", "db"), None),
            P(("groups", "da", "db"), "replica", None),
            P(("groups", "da", "db"), "replica", None),
        ),
        check_vma=False,
    )
```

```python
import functools

import jax
import jax.numpy as jnp
from jax import lax
from jax.experimental import pallas as pl
from jax.experimental.pallas import tpu as pltpu
from jax.sharding import PartitionSpec as P

LANES = 128
ROWS = 16
EXTRA = 8
AXES = ("da", "db")
VMEM_LIMIT = 40 * 1024 * 1024
WHOLE_VMEM = 62 * 1024 * 1024


def silu_parts(projected):
    sigmoid = jax.nn.sigmoid(projected)
    return (projected * sigmoid, sigmoid * (1.0 + projected * (1.0 - sigmoid)))


def body(tokens, grad_out, routes, gates, w_gate_up, w_down):
    local_tokens, features = tokens.shape
    top_count = routes.shape[1]
    hidden_units = w_gate_up.shape[2] // 2
    first_size = lax.axis_size("da")
    second_size = lax.axis_size("db")
    experts = first_size * second_size
    per_round = experts // top_count
    rounds = local_tokens // per_round
    expert_ids = lax.broadcasted_iota(jnp.int32, (1, 1, 1, experts), 3)
    matches = routes.reshape(rounds, per_round, top_count, 1) == expert_ids
    gate_values = gates.reshape(rounds, per_round, top_count, 1).astype(jnp.float32)
    gate_table = jnp.sum(jnp.where(matches, gate_values, 0.0), axis=(1, 2)).astype(jnp.bfloat16)
    chosen = jnp.any(matches, axis=2).astype(jnp.bfloat16)
    input_send = jnp.einsum(
        "rge,rgd->red",
        chosen,
        tokens.reshape(rounds, per_round, features),
        preferred_element_type=jnp.float32,
    ).astype(jnp.bfloat16)
    upstream_send = jnp.einsum(
        "rge,rgd->red",
        chosen,
        grad_out.reshape(rounds, per_round, features),
        preferred_element_type=jnp.float32,
    ).astype(jnp.bfloat16)
    input_recv, upstream_recv, gate_recv = (
        lax.all_to_all(input_send, ("da", "db"), split_axis=1, concat_axis=1, tiled=True),
        lax.all_to_all(upstream_send, ("da", "db"), split_axis=1, concat_axis=1, tiled=True),
        lax.all_to_all(gate_table, ("da", "db"), split_axis=1, concat_axis=1, tiled=True),
    )
    input_rows = input_recv.reshape(-1, features)
    upstream_rows = upstream_recv.reshape(-1, features)
    gate_rows = gate_recv.reshape(-1, 1).astype(jnp.float32)
    w_in, w_out = (
        lax.all_gather(w_gate_up[0], "replica", axis=0, tiled=True),
        lax.all_gather(w_down[0], "replica", axis=0, tiled=True),
    )
    projected = jnp.dot(input_rows, w_in, preferred_element_type=jnp.float32)
    back_raw = jnp.einsum("rd,fd->rf", upstream_rows, w_out, preferred_element_type=jnp.float32)
    gate_part = projected[:, :hidden_units]
    up_part = projected[:, hidden_units:]
    activated, derivative = silu_parts(gate_part)
    hidden = (activated * up_part).astype(jnp.bfloat16)
    gate_scores = jnp.sum(hidden.astype(jnp.float32) * back_raw, axis=1).astype(jnp.bfloat16)
    back_hidden = gate_rows * back_raw
    grad_projected = jnp.concatenate(
        [back_hidden * up_part * derivative, back_hidden * activated], axis=1
    ).astype(jnp.bfloat16)
    scaled_upstream = (gate_rows * upstream_rows.astype(jnp.float32)).astype(jnp.bfloat16)
    input_grads = jnp.einsum("rf,df->rd", grad_projected, w_in, preferred_element_type=jnp.float32)
    input_grads = input_grads.astype(jnp.bfloat16).reshape(rounds, experts, features)
    score_back = gate_scores.reshape(rounds, experts)
    returned, score_ret = (
        lax.all_to_all(input_grads, ("da", "db"), split_axis=1, concat_axis=1, tiled=True),
        lax.all_to_all(score_back, ("da", "db"), split_axis=1, concat_axis=1, tiled=True),
    )
    score_ret = score_ret.reshape(rounds, 1, 1, experts).astype(jnp.float32)
    token_grads = (
        jnp.einsum("rge,red->rgd", chosen, returned, preferred_element_type=jnp.float32)
        .astype(jnp.bfloat16)
        .reshape(local_tokens, features)
    )
    gate_grads = (
        jnp.sum(jnp.where(matches, score_ret, 0.0), axis=3)
        .astype(jnp.bfloat16)
        .reshape(local_tokens, top_count)
    )
    columns = input_rows
    grad_in = lax.psum_scatter(
        jnp.einsum("rd,rf->df", columns, grad_projected, preferred_element_type=jnp.float32).astype(
            jnp.bfloat16
        ),
        "replica",
        scatter_dimension=0,
        tiled=True,
    )
    columns = hidden
    grad_down = lax.psum_scatter(
        jnp.einsum(
            "rf,rd->fd", columns, scaled_upstream, preferred_element_type=jnp.float32
        ).astype(jnp.bfloat16),
        "replica",
        scatter_dimension=0,
        tiled=True,
    )
    return (token_grads, gate_grads, grad_in[None], grad_down[None])


def dot(a, b, contract):
    return lax.dot_general(a, b, ((contract[:1], contract[1:]), ((), ())), preferred_element_type=jnp.float32)


def one_hot(table, expert, rounds, per_round):
    experts, count = table.shape
    rows = lax.broadcasted_iota(jnp.int32, (experts, count), 0)
    line = jnp.sum(jnp.where(rows == expert, table, 0.0), axis=0, keepdims=True)
    token_block = lax.broadcasted_iota(jnp.int32, (rounds, count), 1) // per_round
    mine = lax.broadcasted_iota(jnp.int32, (rounds, count), 0) == token_block
    return jnp.where(mine, line, 0.0)


def fold(table, lanes):
    experts, count = table.shape
    parts = [table[k : k + EXTRA] for k in range(0, experts, EXTRA)]
    used = count * len(parts)
    if used < lanes:
        parts.append(jnp.zeros((EXTRA, lanes - used), table.dtype))
    return jnp.concatenate(parts, axis=1)


def unfold(rows, experts, count):
    return jnp.concatenate([rows[:, k * count : (k + 1) * count] for k in range(experts // EXTRA)], axis=0)


def prepare_kernel(experts, token_hbm, grad_hbm, route_hbm, gate_hbm, out_ref, route_ref, gate_ref, sems):
    local, features = token_hbm.shape
    moves = (
        (route_hbm, route_ref),
        (gate_hbm, gate_ref),
        (token_hbm, out_ref.at[pl.ds(0, local)]),
        (grad_hbm, out_ref.at[pl.ds(local, local)]),
    )
    copies = [pltpu.make_async_copy(source, target, sems.at[k]) for k, (source, target) in enumerate(moves)]
    for copy in copies:
        copy.start()
    for copy in copies[:2]:
        copy.wait()
    routes, gates = route_ref[...], gate_ref[...].astype(jnp.float32)
    ids = lax.broadcasted_iota(jnp.int32, (experts, local), 0)
    table = jnp.zeros((experts, local), jnp.float32)
    for k in range(routes.shape[0]):
        table += jnp.where(routes[k : k + 1] == ids, gates[k : k + 1], 0.0)
    out_ref[2 * local :, :] = fold(table, features).astype(jnp.bfloat16)
    for copy in copies[2:]:
        copy.wait()


def finish_kernel(experts, *refs):
    route_ref, terms, (token_ref, gate_ref) = refs[0], refs[1:-2], refs[-2:]
    local = token_ref.shape[0]
    total = sum(term[...].astype(jnp.float32) for term in terms)
    token_ref[...] = total[:local].astype(jnp.bfloat16)
    scores = unfold(total[local:], experts, local)
    routes = route_ref[...]
    ids = lax.broadcasted_iota(jnp.int32, (experts, local), 0)
    lines = [
        jnp.sum(jnp.where(routes[k : k + 1] == ids, scores, 0.0), axis=0, keepdims=True)
        for k in range(routes.shape[0])
    ]
    gate_ref[...] = jnp.concatenate(lines, axis=0).astype(jnp.bfloat16)


def select_kernel(experts, rounds, per_round, ids_ref, *refs):
    count = (len(refs) - 2) // 2
    shards, (own_ref, other_ref), chosen_refs = refs[:count], refs[count : count + 2], refs[count + 2 :]
    local = rounds * per_round
    for j in range(count):
        features = shards[j].shape[1]
        table = unfold(shards[j][2 * local :, :].astype(jnp.float32), experts, local)
        own = one_hot(table, ids_ref[0], rounds, per_round)
        other = one_hot(table, ids_ref[1], rounds, per_round)
        weights = jnp.concatenate([own, other], axis=0)
        chosen = jnp.where(weights != 0.0, 1.0, 0.0).astype(jnp.bfloat16)
        chosen_refs[j][...] = chosen
        gate = jnp.sum(weights, axis=1, keepdims=True).astype(jnp.bfloat16)
        gate = jnp.broadcast_to(gate, (2 * rounds, LANES))
        for part in range(2):
            picked = dot(chosen, shards[j][part * local : (part + 1) * local, :], (1, 0)).astype(jnp.bfloat16)
            for k, out in ((0, own_ref), (1, other_ref)):
                lines = slice(j * rounds, (j + 1) * rounds)
                half = slice(k * rounds, (k + 1) * rounds)
                out[lines, part * features : (part + 1) * features] = picked[half]
                out[lines, 2 * features :] = gate[half]


def expert_kernel(split, ids_ref, own_ref, other_ref, w_in_ref, w_out_ref, grad_own, grad_other, *kept_refs):
    x_ref, hid_ref, proj_ref, up_ref = kept_refs
    features, double = w_in_ref.shape
    hidden_units = double // 2
    size = own_ref.shape[0]
    w_in, w_out = w_in_ref[...], w_out_ref[...]
    both = ((own_ref, grad_own), (other_ref, grad_other))
    start = 0
    for part in [[pair] for pair in both] if split else [both]:
        rows = size * len(part)
        lines = slice(start, start + rows)
        start += rows

        def taken(begin, end):
            return jnp.concatenate([ref[:, begin:end] for ref, _ in part], axis=0)

        x, upstream = taken(0, features), taken(features, 2 * features)
        gate = taken(2 * features, 2 * features + 1).astype(jnp.float32)
        projected = dot(x, w_in, (1, 0))
        back_raw = dot(upstream, w_out, (1, 1))
        gate_part, up_part = projected[:, :hidden_units], projected[:, hidden_units:]
        activated, derivative = silu_parts(gate_part)
        hidden = (activated * up_part).astype(jnp.bfloat16)
        score = jnp.sum(hidden.astype(jnp.float32) * back_raw, axis=1, keepdims=True)
        back_hidden = gate * back_raw
        grad_projected = jnp.concatenate(
            [back_hidden * up_part * derivative, back_hidden * activated], axis=1
        ).astype(jnp.bfloat16)
        x_ref[lines, :] = x
        hid_ref[lines, :] = hidden
        proj_ref[lines, :] = grad_projected
        up_ref[lines, :] = (gate * upstream.astype(jnp.float32)).astype(jnp.bfloat16)
        input_grad = dot(grad_projected, w_in, (1, 1)).astype(jnp.bfloat16)
        lane = lax.broadcasted_iota(jnp.int32, (rows, LANES), 1)
        scores = jnp.where(lane == ids_ref[0], score, 0.0).astype(jnp.bfloat16)
        for i, (_, out) in enumerate(part):
            out[:, :features] = input_grad[i * size : (i + 1) * size]
            out[:, features:] = scores[i * size : (i + 1) * size]


def spread_kernel(experts, rounds, own_ref, other_ref, *refs):
    count = len(refs) // 2
    chosen_refs, outs = refs[:count], refs[count:]
    for j in range(count):
        lines = slice(j * rounds, (j + 1) * rounds)
        chosen = chosen_refs[j][...]
        local, features = chosen.shape[1], outs[j].shape[1]
        grads = jnp.concatenate([own_ref[lines, :], other_ref[lines, :]], axis=0)
        outs[j][:local, :] = dot(chosen, grads[:, :features], (0, 0)).astype(jnp.bfloat16)
        scores = dot(grads[:, features:], chosen, (0, 0))[:experts]
        outs[j][local:, :] = fold(scores, features).astype(jnp.bfloat16)


def weights_kernel(begun, *refs):
    sums, groups, outs = refs[: 2 * begun], refs[2 * begun : -2], refs[-2:]
    for k, (left, right) in enumerate(((0, 2), (1, 3))):
        total = sums[k][...] if begun else None
        for g in range(0, len(groups), 4):
            part = dot(groups[g + left][...], groups[g + right][...], (0, 0))
            total = part if total is None else total + part
        if begun:
            outs[k][0] = total.astype(jnp.bfloat16)
        else:
            outs[k][...] = total


def call(kernel, outs, args, smem=0, hbm=0, scratch=(), dtype=jnp.bfloat16, flops=0, vmem=VMEM_LIMIT):
    in_specs = [pl.BlockSpec(memory_space=pltpu.SMEM)] * smem
    in_specs += [pl.BlockSpec(memory_space=pltpu.HBM)] * hbm
    in_specs += [pl.BlockSpec(memory_space=pltpu.VMEM)] * (len(args) - smem - hbm)
    return pl.pallas_call(
        kernel,
        out_shape=[jax.ShapeDtypeStruct(s, dtype) for s in outs],
        in_specs=in_specs,
        out_specs=[pl.BlockSpec(memory_space=pltpu.VMEM)] * len(outs),
        scratch_shapes=scratch,
        compiler_params=pltpu.CompilerParams(vmem_limit_bytes=vmem),
        cost_estimate=pl.CostEstimate(flops=flops, bytes_accessed=1 << 20, transcendentals=0),
    )(*args)


def ring_body(sizes, tokens, grad_out, routes, gates, w_gate_up, w_down):
    first_size, second_size = sizes
    local, features = tokens.shape
    top_count = routes.shape[1]
    experts = first_size * second_size
    per_round = experts // top_count
    rounds = local // per_round
    hidden_units = w_gate_up.shape[2] // 2
    ring = [(0, z) for z in range(second_size)] + [(1, z) for z in reversed(range(second_size))]
    length = len(ring)
    half = length // 2

    def device(place, core):
        x, z = ring[place % length]
        return (x * 2 + core) * second_size + z

    def shift(value, step):
        pairs = [(device(p, c), device(p + (step if c == 0 else -step), c)) for p in range(length) for c in range(2)]
        return lax.ppermute(value, AXES, pairs)

    def swap(value):
        pairs = [(device(p, c), device(p, 1 - c)) for p in range(length) for c in range(2)]
        return lax.ppermute(value, AXES, pairs)

    me, row = lax.axis_index("da"), lax.axis_index("db")
    core = lax.rem(me, 2)
    ids = jnp.stack([me * second_size + row, (me + 1 - 2 * core) * second_size + row]).astype(jnp.int32)

    (message,) = call(
        functools.partial(prepare_kernel, experts),
        [(2 * local + EXTRA, features)],
        [tokens, grad_out, routes.T, gates.T],
        hbm=4,
        vmem=WHOLE_VMEM,
        scratch=[
            pltpu.VMEM((top_count, local), routes.dtype),
            pltpu.VMEM((top_count, local), gates.dtype),
            pltpu.SemaphoreType.DMA((4,)),
        ],
    )
    mine, theirs = {0: message}, {}
    mine[1] = shift(mine[0], 1)
    theirs[0] = swap(mine[0])
    theirs[1] = shift(theirs[0], 1)
    w_in, w_out = w_gate_up[0], w_down[0]
    own_sums, other_sums = {}, {}

    def work(group):
        size = len(group) * rounds
        shards = [(mine if own else theirs)[k] for own, k in group]
        own, other, *chosen = call(
            functools.partial(select_kernel, experts, rounds, per_round),
            [(size, 2 * features + LANES)] * 2 + [(2 * rounds, local)] * len(group),
            [ids] + shards,
            smem=1,
            flops=8 * 4 * size * local * 2 * features,
        )
        other = swap(other)
        own_grad, other_grad, *kept = call(
            functools.partial(expert_kernel, size > LANES),
            [(size, features + LANES)] * 2
            + [(2 * size, n) for n in (features, hidden_units, 2 * hidden_units, features)],
            [ids, own, other, w_in, w_out],
            smem=1,
            flops=10 * 2 * 2 * size * features * 5 * hidden_units,
        )
        other_grad = swap(other_grad)
        spread = call(
            functools.partial(spread_kernel, experts, rounds),
            [(local + EXTRA, features)] * len(group),
            [own_grad, other_grad] + chosen,
            flops=8 * 4 * size * local * features,
        )
        for (own, k), total in zip(group, spread):
            (own_sums if own else other_sums)[k] = total
        return kept

    def after(value, *earlier):
        return lax.optimization_barrier((value, *earlier))[0]

    groups = [[(True, 0), (True, 1), (False, 1)]]
    groups += [[(True, k), (False, k)] for k in range(2, half)] + [[(True, half)]]
    kept, early = [], []
    for k, group in enumerate(groups, 1):
        if k < half:
            mine[k + 1] = shift(mine[k], 1)
            if k + 1 < half:
                theirs[k + 1] = shift(theirs[k], 1)
        if k == half - 1:
            early = call(
                functools.partial(weights_kernel, False),
                [(features, 2 * hidden_units), (hidden_units, features)],
                kept,
                dtype=jnp.float32,
                flops=10 * 2 * sum(x.shape[0] for x in kept[::4]) * features * 3 * hidden_units,
            )
            kept = []
        if k == half:
            mine[half] = after(mine[half], *early, *[v for k, v in own_sums.items() if k < half - 1], *[v for k, v in other_sums.items() if k < half - 1])
        kept += work(group)

    def add(*terms):
        return sum(t.astype(jnp.float32) for t in terms).astype(jnp.bfloat16)

    there, here = other_sums[half - 1], own_sums[half]
    for k in range(half - 1, 0, -1):
        there = shift(there, -1)
        here = add(shift(here, -1), own_sums[k])
        if k > 1:
            there = add(there, other_sums[k - 1])
    token_grads, gate_grads = call(
        functools.partial(finish_kernel, experts),
        [(local, features), (top_count, local)],
        [routes.T, own_sums[0], swap(there), shift(here, -1)],
    )

    grad_in, grad_down = call(
        functools.partial(weights_kernel, True),
        [(1, features, 2 * hidden_units), (1, hidden_units, features)],
        list(early) + kept,
        smem=0,
        flops=10 * 2 * sum(x.shape[0] for x in kept[::4]) * features * 3 * hidden_units,
    )
    return token_grads, gate_grads.T, grad_in, grad_down


def solution(mesh):
    placed = (
        P(("groups", "replica", "da", "db"), None),
        P(("groups", "replica", "da", "db"), None),
        P(("groups", "replica", "da", "db"), None),
        P(("groups", "replica", "da", "db"), None),
        P(("da", "db"), "replica", None),
        P(("da", "db"), "replica", None),
    )
    first_size, second_size = mesh.shape["da"], mesh.shape["db"]
    experts = first_size * second_size

    def chosen_body(tokens, grad_out, routes, gates, w_gate_up, w_down):
        local, top_count = routes.shape
        dense = experts // top_count <= 2
        closed = mesh.shape["replica"] == 1 and first_size == 4 and second_size >= 2
        fits = local % LANES == 0 and experts % ROWS == 0 and experts <= LANES
        fits = fits and experts * local <= EXTRA * tokens.shape[1] and (local * top_count // experts) % ROWS == 0
        args = (tokens, grad_out, routes, gates, w_gate_up, w_down)
        if dense and closed and fits:
            return ring_body((first_size, second_size), *args)
        return body(*args)

    return jax.shard_map(
        chosen_body,
        mesh=mesh,
        in_specs=placed,
        out_specs=(
            P(("groups", "replica", "da", "db"), None),
            P(("groups", "replica", "da", "db"), None),
            P(("groups", "da", "db"), "replica", None),
            P(("groups", "da", "db"), "replica", None),
        ),
        check_vma=False,
    )
```

```python
import functools

import jax
import jax.numpy as jnp
from jax import lax
from jax.experimental import pallas as pl
from jax.experimental.pallas import tpu as pltpu
from jax.sharding import PartitionSpec as P

LANES = 128
ROWS = 16
EXTRA = 8
AXES = ("da", "db")
VMEM_LIMIT = 40 * 1024 * 1024
WHOLE_VMEM = 62 * 1024 * 1024


def silu_parts(projected):
    sigmoid = jax.nn.sigmoid(projected)
    return (projected * sigmoid, sigmoid * (1.0 + projected * (1.0 - sigmoid)))


def body(tokens, grad_out, routes, gates, w_gate_up, w_down):
    local_tokens, features = tokens.shape
    top_count = routes.shape[1]
    hidden_units = w_gate_up.shape[2] // 2
    first_size = lax.axis_size("da")
    second_size = lax.axis_size("db")
    experts = first_size * second_size
    per_round = experts // top_count
    rounds = local_tokens // per_round
    expert_ids = lax.broadcasted_iota(jnp.int32, (1, 1, 1, experts), 3)
    matches = routes.reshape(rounds, per_round, top_count, 1) == expert_ids
    gate_values = gates.reshape(rounds, per_round, top_count, 1).astype(jnp.float32)
    gate_table = jnp.sum(jnp.where(matches, gate_values, 0.0), axis=(1, 2)).astype(jnp.bfloat16)
    chosen = jnp.any(matches, axis=2).astype(jnp.bfloat16)
    input_send = jnp.einsum(
        "rge,rgd->red",
        chosen,
        tokens.reshape(rounds, per_round, features),
        preferred_element_type=jnp.float32,
    ).astype(jnp.bfloat16)
    upstream_send = jnp.einsum(
        "rge,rgd->red",
        chosen,
        grad_out.reshape(rounds, per_round, features),
        preferred_element_type=jnp.float32,
    ).astype(jnp.bfloat16)
    input_recv, upstream_recv, gate_recv = (
        lax.all_to_all(input_send, ("da", "db"), split_axis=1, concat_axis=1, tiled=True),
        lax.all_to_all(upstream_send, ("da", "db"), split_axis=1, concat_axis=1, tiled=True),
        lax.all_to_all(gate_table, ("da", "db"), split_axis=1, concat_axis=1, tiled=True),
    )
    input_rows = input_recv.reshape(-1, features)
    upstream_rows = upstream_recv.reshape(-1, features)
    gate_rows = gate_recv.reshape(-1, 1).astype(jnp.float32)
    w_in, w_out = (
        lax.all_gather(w_gate_up[0], "replica", axis=0, tiled=True),
        lax.all_gather(w_down[0], "replica", axis=0, tiled=True),
    )
    projected = jnp.dot(input_rows, w_in, preferred_element_type=jnp.float32)
    back_raw = jnp.einsum("rd,fd->rf", upstream_rows, w_out, preferred_element_type=jnp.float32)
    gate_part = projected[:, :hidden_units]
    up_part = projected[:, hidden_units:]
    activated, derivative = silu_parts(gate_part)
    hidden = (activated * up_part).astype(jnp.bfloat16)
    gate_scores = jnp.sum(hidden.astype(jnp.float32) * back_raw, axis=1).astype(jnp.bfloat16)
    back_hidden = gate_rows * back_raw
    grad_projected = jnp.concatenate(
        [back_hidden * up_part * derivative, back_hidden * activated], axis=1
    ).astype(jnp.bfloat16)
    scaled_upstream = (gate_rows * upstream_rows.astype(jnp.float32)).astype(jnp.bfloat16)
    input_grads = jnp.einsum("rf,df->rd", grad_projected, w_in, preferred_element_type=jnp.float32)
    input_grads = input_grads.astype(jnp.bfloat16).reshape(rounds, experts, features)
    score_back = gate_scores.reshape(rounds, experts)
    returned, score_ret = (
        lax.all_to_all(input_grads, ("da", "db"), split_axis=1, concat_axis=1, tiled=True),
        lax.all_to_all(score_back, ("da", "db"), split_axis=1, concat_axis=1, tiled=True),
    )
    score_ret = score_ret.reshape(rounds, 1, 1, experts).astype(jnp.float32)
    token_grads = (
        jnp.einsum("rge,red->rgd", chosen, returned, preferred_element_type=jnp.float32)
        .astype(jnp.bfloat16)
        .reshape(local_tokens, features)
    )
    gate_grads = (
        jnp.sum(jnp.where(matches, score_ret, 0.0), axis=3)
        .astype(jnp.bfloat16)
        .reshape(local_tokens, top_count)
    )
    columns = input_rows
    grad_in = lax.psum_scatter(
        jnp.einsum("rd,rf->df", columns, grad_projected, preferred_element_type=jnp.float32).astype(
            jnp.bfloat16
        ),
        "replica",
        scatter_dimension=0,
        tiled=True,
    )
    columns = hidden
    grad_down = lax.psum_scatter(
        jnp.einsum(
            "rf,rd->fd", columns, scaled_upstream, preferred_element_type=jnp.float32
        ).astype(jnp.bfloat16),
        "replica",
        scatter_dimension=0,
        tiled=True,
    )
    return (token_grads, gate_grads, grad_in[None], grad_down[None])


def dot(a, b, contract):
    return lax.dot_general(a, b, ((contract[:1], contract[1:]), ((), ())), preferred_element_type=jnp.float32)


def one_hot(table, expert, rounds, per_round):
    experts, count = table.shape
    rows = lax.broadcasted_iota(jnp.int32, (experts, count), 0)
    line = jnp.sum(jnp.where(rows == expert, table, 0.0), axis=0, keepdims=True)
    token_block = lax.broadcasted_iota(jnp.int32, (rounds, count), 1) // per_round
    mine = lax.broadcasted_iota(jnp.int32, (rounds, count), 0) == token_block
    return jnp.where(mine, line, 0.0)


def fold(table, lanes):
    experts, count = table.shape
    parts = [table[k : k + EXTRA] for k in range(0, experts, EXTRA)]
    used = count * len(parts)
    if used < lanes:
        parts.append(jnp.zeros((EXTRA, lanes - used), table.dtype))
    return jnp.concatenate(parts, axis=1)


def unfold(rows, experts, count):
    return jnp.concatenate([rows[:, k * count : (k + 1) * count] for k in range(experts // EXTRA)], axis=0)


def prepare_kernel(experts, token_hbm, grad_hbm, route_hbm, gate_hbm, out_ref, route_ref, gate_ref, sems):
    local, features = token_hbm.shape
    moves = (
        (route_hbm, route_ref),
        (gate_hbm, gate_ref),
        (token_hbm, out_ref.at[pl.ds(0, local)]),
        (grad_hbm, out_ref.at[pl.ds(local, local)]),
    )
    copies = [pltpu.make_async_copy(source, target, sems.at[k]) for k, (source, target) in enumerate(moves)]
    for copy in copies:
        copy.start()
    for copy in copies[:2]:
        copy.wait()
    routes, gates = route_ref[...], gate_ref[...].astype(jnp.float32)
    ids = lax.broadcasted_iota(jnp.int32, (experts, local), 0)
    table = jnp.zeros((experts, local), jnp.float32)
    for k in range(routes.shape[0]):
        table += jnp.where(routes[k : k + 1] == ids, gates[k : k + 1], 0.0)
    out_ref[2 * local :, :] = fold(table, features).astype(jnp.bfloat16)
    for copy in copies[2:]:
        copy.wait()


def finish_kernel(experts, *refs):
    route_ref, terms, (token_ref, gate_ref) = refs[0], refs[1:-2], refs[-2:]
    local = token_ref.shape[0]
    total = sum(term[...].astype(jnp.float32) for term in terms)
    token_ref[...] = total[:local].astype(jnp.bfloat16)
    scores = unfold(total[local:], experts, local)
    routes = route_ref[...]
    ids = lax.broadcasted_iota(jnp.int32, (experts, local), 0)
    lines = [
        jnp.sum(jnp.where(routes[k : k + 1] == ids, scores, 0.0), axis=0, keepdims=True)
        for k in range(routes.shape[0])
    ]
    gate_ref[...] = jnp.concatenate(lines, axis=0).astype(jnp.bfloat16)


def select_kernel(experts, rounds, per_round, ids_ref, *refs):
    count = (len(refs) - 2) // 2
    shards, (own_ref, other_ref), chosen_refs = refs[:count], refs[count : count + 2], refs[count + 2 :]
    local = rounds * per_round
    for j in range(count):
        features = shards[j].shape[1]
        table = unfold(shards[j][2 * local :, :].astype(jnp.float32), experts, local)
        own = one_hot(table, ids_ref[0], rounds, per_round)
        other = one_hot(table, ids_ref[1], rounds, per_round)
        weights = jnp.concatenate([own, other], axis=0)
        chosen = jnp.where(weights != 0.0, 1.0, 0.0).astype(jnp.bfloat16)
        chosen_refs[j][...] = chosen
        gate = jnp.sum(weights, axis=1, keepdims=True).astype(jnp.bfloat16)
        gate = jnp.broadcast_to(gate, (2 * rounds, LANES))
        for part in range(2):
            picked = dot(chosen, shards[j][part * local : (part + 1) * local, :], (1, 0)).astype(jnp.bfloat16)
            for k, out in ((0, own_ref), (1, other_ref)):
                lines = slice(j * rounds, (j + 1) * rounds)
                half = slice(k * rounds, (k + 1) * rounds)
                out[lines, part * features : (part + 1) * features] = picked[half]
                out[lines, 2 * features :] = gate[half]


def expert_kernel(split, ids_ref, own_ref, other_ref, w_in_ref, back_in_ref, back_out_ref, grad_own, grad_other, *kept_refs):
    x_ref, hid_ref, proj_ref, up_ref = kept_refs
    features, double = w_in_ref.shape
    hidden_units = double // 2
    size = own_ref.shape[0]
    w_in, back_in, back_out = w_in_ref[...], back_in_ref[...], back_out_ref[...]
    both = ((own_ref, grad_own), (other_ref, grad_other))
    start = 0
    for part in [[pair] for pair in both] if split else [both]:
        rows = size * len(part)
        lines = slice(start, start + rows)
        start += rows

        def taken(begin, end):
            return jnp.concatenate([ref[:, begin:end] for ref, _ in part], axis=0)

        x, upstream = taken(0, features), taken(features, 2 * features)
        gate = taken(2 * features, 2 * features + 1).astype(jnp.float32)
        projected = dot(x, w_in, (1, 0))
        back_raw = dot(upstream, back_out, (1, 0))
        gate_part, up_part = projected[:, :hidden_units], projected[:, hidden_units:]
        activated, derivative = silu_parts(gate_part)
        hidden = (activated * up_part).astype(jnp.bfloat16)
        score = jnp.sum(hidden.astype(jnp.float32) * back_raw, axis=1, keepdims=True)
        back_hidden = gate * back_raw
        grad_projected = jnp.concatenate(
            [back_hidden * up_part * derivative, back_hidden * activated], axis=1
        ).astype(jnp.bfloat16)
        x_ref[lines, :] = x
        hid_ref[lines, :] = hidden
        proj_ref[lines, :] = grad_projected
        up_ref[lines, :] = (gate * upstream.astype(jnp.float32)).astype(jnp.bfloat16)
        input_grad = dot(grad_projected, back_in, (1, 0)).astype(jnp.bfloat16)
        lane = lax.broadcasted_iota(jnp.int32, (rows, LANES), 1)
        scores = jnp.where(lane == ids_ref[0], score, 0.0).astype(jnp.bfloat16)
        for i, (_, out) in enumerate(part):
            out[:, :features] = input_grad[i * size : (i + 1) * size]
            out[:, features:] = scores[i * size : (i + 1) * size]


def transpose_kernel(*refs):
    for source, target in zip(refs[: len(refs) // 2], refs[len(refs) // 2 :]):
        target[...] = source[...].T


def spread_kernel(experts, rounds, own_ref, other_ref, *refs):
    count = len(refs) // 2
    chosen_refs, outs = refs[:count], refs[count:]
    for j in range(count):
        lines = slice(j * rounds, (j + 1) * rounds)
        chosen = chosen_refs[j][...]
        local, features = chosen.shape[1], outs[j].shape[1]
        grads = jnp.concatenate([own_ref[lines, :], other_ref[lines, :]], axis=0)
        outs[j][:local, :] = dot(chosen, grads[:, :features], (0, 0)).astype(jnp.bfloat16)
        scores = dot(grads[:, features:], chosen, (0, 0))[:experts]
        outs[j][local:, :] = fold(scores, features).astype(jnp.bfloat16)


def weights_kernel(begun, *refs):
    sums, groups, outs = refs[: 2 * begun], refs[2 * begun : -2], refs[-2:]
    for k, (left, right) in enumerate(((0, 2), (1, 3))):
        total = sums[k][...] if begun else None
        for g in range(0, len(groups), 4):
            part = dot(groups[g + left][...], groups[g + right][...], (0, 0))
            total = part if total is None else total + part
        if begun:
            outs[k][0] = total.astype(jnp.bfloat16)
        else:
            outs[k][...] = total


def call(kernel, outs, args, smem=0, hbm=0, scratch=(), dtype=jnp.bfloat16, flops=0, vmem=VMEM_LIMIT):
    in_specs = [pl.BlockSpec(memory_space=pltpu.SMEM)] * smem
    in_specs += [pl.BlockSpec(memory_space=pltpu.HBM)] * hbm
    in_specs += [pl.BlockSpec(memory_space=pltpu.VMEM)] * (len(args) - smem - hbm)
    return pl.pallas_call(
        kernel,
        out_shape=[jax.ShapeDtypeStruct(s, dtype) for s in outs],
        in_specs=in_specs,
        out_specs=[pl.BlockSpec(memory_space=pltpu.VMEM)] * len(outs),
        scratch_shapes=scratch,
        compiler_params=pltpu.CompilerParams(vmem_limit_bytes=vmem),
        cost_estimate=pl.CostEstimate(flops=flops, bytes_accessed=1 << 20, transcendentals=0),
    )(*args)


def ring_body(sizes, tokens, grad_out, routes, gates, w_gate_up, w_down):
    first_size, second_size = sizes
    local, features = tokens.shape
    top_count = routes.shape[1]
    experts = first_size * second_size
    per_round = experts // top_count
    rounds = local // per_round
    hidden_units = w_gate_up.shape[2] // 2
    ring = [(0, z) for z in range(second_size)] + [(1, z) for z in reversed(range(second_size))]
    length = len(ring)
    half = length // 2

    def device(place, core):
        x, z = ring[place % length]
        return (x * 2 + core) * second_size + z

    def shift(value, step):
        pairs = [(device(p, c), device(p + (step if c == 0 else -step), c)) for p in range(length) for c in range(2)]
        return lax.ppermute(value, AXES, pairs)

    def swap(value):
        pairs = [(device(p, c), device(p, 1 - c)) for p in range(length) for c in range(2)]
        return lax.ppermute(value, AXES, pairs)

    me, row = lax.axis_index("da"), lax.axis_index("db")
    core = lax.rem(me, 2)
    ids = jnp.stack([me * second_size + row, (me + 1 - 2 * core) * second_size + row]).astype(jnp.int32)

    (message,) = call(
        functools.partial(prepare_kernel, experts),
        [(2 * local + EXTRA, features)],
        [tokens, grad_out, routes.T, gates.T],
        hbm=4,
        vmem=WHOLE_VMEM,
        scratch=[
            pltpu.VMEM((top_count, local), routes.dtype),
            pltpu.VMEM((top_count, local), gates.dtype),
            pltpu.SemaphoreType.DMA((4,)),
        ],
    )
    mine, theirs = {0: message}, {}
    mine[1] = shift(mine[0], 1)
    theirs[0] = swap(mine[0])
    theirs[1] = shift(theirs[0], 1)

    def after(value, *earlier):
        return lax.optimization_barrier((value, *earlier))[0]

    w_in, w_out = w_gate_up[0], w_down[0]
    back_in, back_out = call(transpose_kernel, [w.shape[::-1] for w in (w_in, w_out)], [w_in, w_out])
    mine[1] = after(mine[1], back_in, back_out)
    own_sums, other_sums = {}, {}

    def pick(group, *earlier):
        size = len(group) * rounds
        shards = [(mine if own else theirs)[k] for own, k in group]
        if earlier:
            shards[-1] = after(shards[-1], *earlier)
        own, other, *chosen = call(
            functools.partial(select_kernel, experts, rounds, per_round),
            [(size, 2 * features + LANES)] * 2 + [(2 * rounds, local)] * len(group),
            [ids] + shards,
            smem=1,
            flops=8 * 4 * size * local * 2 * features,
        )
        return group, size, own, swap(other), chosen

    def work(picked):
        group, size, own, other, chosen = picked
        own_grad, other_grad, *kept = call(
            functools.partial(expert_kernel, size > LANES),
            [(size, features + LANES)] * 2
            + [(2 * size, n) for n in (features, hidden_units, 2 * hidden_units, features)],
            [ids, own, other, w_in, back_in, back_out],
            smem=1,
            flops=10 * 2 * 2 * size * features * 5 * hidden_units,
        )
        other_grad = swap(other_grad)
        spread = call(
            functools.partial(spread_kernel, experts, rounds),
            [(local + EXTRA, features)] * len(group),
            [own_grad, other_grad] + chosen,
            flops=8 * 4 * size * local * features,
        )
        for (own, k), total in zip(group, spread):
            (own_sums if own else other_sums)[k] = total
        return kept

    for k in range(1, half):
        mine[k + 1] = shift(mine[k], 1)
        if k + 1 < half:
            theirs[k + 1] = shift(theirs[k], 1)

    near = [[(True, 0), (True, 1), (False, 1)]] + [[(True, k), (False, k)] for k in range(2, half - 1)]
    kept = [array for group in near for array in work(pick(group))]
    done = [*own_sums.values(), *other_sums.values()]
    early = call(
        functools.partial(weights_kernel, False),
        [(features, 2 * hidden_units), (hidden_units, features)],
        kept,
        dtype=jnp.float32,
        flops=10 * 2 * sum(x.shape[0] for x in kept[::4]) * features * 3 * hidden_units,
    )
    kept = work(pick([(True, half - 1), (False, half - 1)]))
    kept = kept + work(pick([(True, half)], *done, kept[0]))

    def add(*terms):
        return sum(t.astype(jnp.float32) for t in terms).astype(jnp.bfloat16)

    there, here = other_sums[half - 1], own_sums[half - 1]
    far = shift(own_sums[half], -2)
    for k in range(half - 2, -1, -1):
        there, here = shift(there, -1), shift(here, -1)
        if k > 0:
            there = add(there, other_sums[k])
            here = add(here, own_sums[k], far) if k == half - 2 else add(here, own_sums[k])
    token_grads, gate_grads = call(
        functools.partial(finish_kernel, experts),
        [(local, features), (top_count, local)],
        [routes.T, own_sums[0], swap(there), here],
    )

    grad_in, grad_down = call(
        functools.partial(weights_kernel, True),
        [(1, features, 2 * hidden_units), (1, hidden_units, features)],
        list(early) + kept,
        smem=0,
        flops=10 * 2 * sum(x.shape[0] for x in kept[::4]) * features * 3 * hidden_units,
    )
    return token_grads, gate_grads.T, grad_in, grad_down


def solution(mesh):
    placed = (
        P(("groups", "replica", "da", "db"), None),
        P(("groups", "replica", "da", "db"), None),
        P(("groups", "replica", "da", "db"), None),
        P(("groups", "replica", "da", "db"), None),
        P(("da", "db"), "replica", None),
        P(("da", "db"), "replica", None),
    )
    first_size, second_size = mesh.shape["da"], mesh.shape["db"]
    experts = first_size * second_size

    def chosen_body(tokens, grad_out, routes, gates, w_gate_up, w_down):
        local, top_count = routes.shape
        dense = experts // top_count <= 2
        closed = mesh.shape["replica"] == 1 and first_size == 4 and second_size >= 3
        fits = local % LANES == 0 and experts % ROWS == 0 and experts <= LANES
        fits = fits and experts * local <= EXTRA * tokens.shape[1] and (local * top_count // experts) % ROWS == 0
        args = (tokens, grad_out, routes, gates, w_gate_up, w_down)
        if dense and closed and fits:
            return ring_body((first_size, second_size), *args)
        return body(*args)

    return jax.shard_map(
        chosen_body,
        mesh=mesh,
        in_specs=placed,
        out_specs=(
            P(("groups", "replica", "da", "db"), None),
            P(("groups", "replica", "da", "db"), None),
            P(("groups", "da", "db"), "replica", None),
            P(("groups", "da", "db"), "replica", None),
        ),
        check_vma=False,
    )
```

```python
import functools

import jax
import jax.numpy as jnp
from jax import lax
from jax.experimental import pallas as pl
from jax.experimental.pallas import tpu as pltpu
from jax.sharding import PartitionSpec as P

LANES = 128
ROWS = 16
EXTRA = 8
AXES = ("da", "db")
VMEM_LIMIT = 24 * 1024 * 1024
WHOLE_VMEM = 62 * 1024 * 1024


def silu_parts(projected):
    sigmoid = jax.nn.sigmoid(projected)
    return (projected * sigmoid, sigmoid * (1.0 + projected * (1.0 - sigmoid)))


def body(tokens, grad_out, routes, gates, w_gate_up, w_down):
    local_tokens, features = tokens.shape
    top_count = routes.shape[1]
    hidden_units = w_gate_up.shape[2] // 2
    first_size = lax.axis_size("da")
    second_size = lax.axis_size("db")
    experts = first_size * second_size
    per_round = experts // top_count
    rounds = local_tokens // per_round
    expert_ids = lax.broadcasted_iota(jnp.int32, (1, 1, 1, experts), 3)
    matches = routes.reshape(rounds, per_round, top_count, 1) == expert_ids
    gate_values = gates.reshape(rounds, per_round, top_count, 1).astype(jnp.float32)
    gate_table = jnp.sum(jnp.where(matches, gate_values, 0.0), axis=(1, 2)).astype(jnp.bfloat16)
    chosen = jnp.any(matches, axis=2).astype(jnp.bfloat16)
    input_send = jnp.einsum(
        "rge,rgd->red",
        chosen,
        tokens.reshape(rounds, per_round, features),
        preferred_element_type=jnp.float32,
    ).astype(jnp.bfloat16)
    upstream_send = jnp.einsum(
        "rge,rgd->red",
        chosen,
        grad_out.reshape(rounds, per_round, features),
        preferred_element_type=jnp.float32,
    ).astype(jnp.bfloat16)
    input_recv, upstream_recv, gate_recv = (
        lax.all_to_all(input_send, ("da", "db"), split_axis=1, concat_axis=1, tiled=True),
        lax.all_to_all(upstream_send, ("da", "db"), split_axis=1, concat_axis=1, tiled=True),
        lax.all_to_all(gate_table, ("da", "db"), split_axis=1, concat_axis=1, tiled=True),
    )
    input_rows = input_recv.reshape(-1, features)
    upstream_rows = upstream_recv.reshape(-1, features)
    gate_rows = gate_recv.reshape(-1, 1).astype(jnp.float32)
    w_in, w_out = (
        lax.all_gather(w_gate_up[0], "replica", axis=0, tiled=True),
        lax.all_gather(w_down[0], "replica", axis=0, tiled=True),
    )
    projected = jnp.dot(input_rows, w_in, preferred_element_type=jnp.float32)
    back_raw = jnp.einsum("rd,fd->rf", upstream_rows, w_out, preferred_element_type=jnp.float32)
    gate_part = projected[:, :hidden_units]
    up_part = projected[:, hidden_units:]
    activated, derivative = silu_parts(gate_part)
    hidden = (activated * up_part).astype(jnp.bfloat16)
    gate_scores = jnp.sum(hidden.astype(jnp.float32) * back_raw, axis=1).astype(jnp.bfloat16)
    back_hidden = gate_rows * back_raw
    grad_projected = jnp.concatenate(
        [back_hidden * up_part * derivative, back_hidden * activated], axis=1
    ).astype(jnp.bfloat16)
    scaled_upstream = (gate_rows * upstream_rows.astype(jnp.float32)).astype(jnp.bfloat16)
    input_grads = jnp.einsum("rf,df->rd", grad_projected, w_in, preferred_element_type=jnp.float32)
    input_grads = input_grads.astype(jnp.bfloat16).reshape(rounds, experts, features)
    score_back = gate_scores.reshape(rounds, experts)
    returned, score_ret = (
        lax.all_to_all(input_grads, ("da", "db"), split_axis=1, concat_axis=1, tiled=True),
        lax.all_to_all(score_back, ("da", "db"), split_axis=1, concat_axis=1, tiled=True),
    )
    score_ret = score_ret.reshape(rounds, 1, 1, experts).astype(jnp.float32)
    token_grads = (
        jnp.einsum("rge,red->rgd", chosen, returned, preferred_element_type=jnp.float32)
        .astype(jnp.bfloat16)
        .reshape(local_tokens, features)
    )
    gate_grads = (
        jnp.sum(jnp.where(matches, score_ret, 0.0), axis=3)
        .astype(jnp.bfloat16)
        .reshape(local_tokens, top_count)
    )
    columns = input_rows
    grad_in = lax.psum_scatter(
        jnp.einsum("rd,rf->df", columns, grad_projected, preferred_element_type=jnp.float32).astype(
            jnp.bfloat16
        ),
        "replica",
        scatter_dimension=0,
        tiled=True,
    )
    columns = hidden
    grad_down = lax.psum_scatter(
        jnp.einsum(
            "rf,rd->fd", columns, scaled_upstream, preferred_element_type=jnp.float32
        ).astype(jnp.bfloat16),
        "replica",
        scatter_dimension=0,
        tiled=True,
    )
    return (token_grads, gate_grads, grad_in[None], grad_down[None])


def dot(a, b, contract):
    return lax.dot_general(a, b, ((contract[:1], contract[1:]), ((), ())), preferred_element_type=jnp.float32)


def one_hot(table, expert, rounds, per_round):
    experts, count = table.shape
    rows = lax.broadcasted_iota(jnp.int32, (experts, count), 0)
    line = jnp.sum(jnp.where(rows == expert, table, 0.0), axis=0, keepdims=True)
    token_block = lax.broadcasted_iota(jnp.int32, (rounds, count), 1) // per_round
    mine = lax.broadcasted_iota(jnp.int32, (rounds, count), 0) == token_block
    return jnp.where(mine, line, 0.0)


def fold(table, lanes):
    experts, count = table.shape
    parts = [table[k : k + EXTRA] for k in range(0, experts, EXTRA)]
    used = count * len(parts)
    if used < lanes:
        parts.append(jnp.zeros((EXTRA, lanes - used), table.dtype))
    return jnp.concatenate(parts, axis=1)


def unfold(rows, experts, count):
    return jnp.concatenate([rows[:, k * count : (k + 1) * count] for k in range(experts // EXTRA)], axis=0)


def prepare_kernel(experts, token_hbm, grad_hbm, route_hbm, gate_hbm, out_ref, route_ref, gate_ref, sems):
    local, features = token_hbm.shape
    moves = (
        (route_hbm, route_ref),
        (gate_hbm, gate_ref),
        (token_hbm, out_ref.at[pl.ds(0, local)]),
        (grad_hbm, out_ref.at[pl.ds(local, local)]),
    )
    copies = [pltpu.make_async_copy(source, target, sems.at[k]) for k, (source, target) in enumerate(moves)]
    for copy in copies:
        copy.start()
    for copy in copies[:2]:
        copy.wait()
    routes, gates = route_ref[...], gate_ref[...].astype(jnp.float32)
    ids = lax.broadcasted_iota(jnp.int32, (experts, local), 0)
    table = jnp.zeros((experts, local), jnp.float32)
    for k in range(routes.shape[0]):
        table += jnp.where(routes[k : k + 1] == ids, gates[k : k + 1], 0.0)
    out_ref[2 * local :, :] = fold(table, features).astype(jnp.bfloat16)
    for copy in copies[2:]:
        copy.wait()


def finish_kernel(experts, *refs):
    route_ref, terms, (token_ref, gate_ref) = refs[0], refs[1:-2], refs[-2:]
    local = token_ref.shape[0]
    total = sum(term[...].astype(jnp.float32) for term in terms)
    token_ref[...] = total[:local].astype(jnp.bfloat16)
    scores = unfold(total[local:], experts, local)
    routes = route_ref[...]
    ids = lax.broadcasted_iota(jnp.int32, (experts, local), 0)
    lines = [
        jnp.sum(jnp.where(routes[k : k + 1] == ids, scores, 0.0), axis=0, keepdims=True)
        for k in range(routes.shape[0])
    ]
    gate_ref[...] = jnp.concatenate(lines, axis=0).astype(jnp.bfloat16)


def select_kernel(experts, rounds, per_round, ids_ref, *refs):
    count = (len(refs) - 2) // 2
    shards, (own_ref, other_ref), chosen_refs = refs[:count], refs[count : count + 2], refs[count + 2 :]
    local = rounds * per_round
    for j in range(count):
        features = shards[j].shape[1]
        table = unfold(shards[j][2 * local :, :].astype(jnp.float32), experts, local)
        own = one_hot(table, ids_ref[0], rounds, per_round)
        other = one_hot(table, ids_ref[1], rounds, per_round)
        weights = jnp.concatenate([own, other], axis=0)
        chosen = jnp.where(weights != 0.0, 1.0, 0.0).astype(jnp.bfloat16)
        chosen_refs[j][...] = chosen
        gate = jnp.sum(weights, axis=1, keepdims=True).astype(jnp.bfloat16)
        gate = jnp.broadcast_to(gate, (2 * rounds, LANES))
        for part in range(2):
            picked = dot(chosen, shards[j][part * local : (part + 1) * local, :], (1, 0)).astype(jnp.bfloat16)
            for k, out in ((0, own_ref), (1, other_ref)):
                lines = slice(j * rounds, (j + 1) * rounds)
                half = slice(k * rounds, (k + 1) * rounds)
                out[lines, part * features : (part + 1) * features] = picked[half]
                out[lines, 2 * features :] = gate[half]


def expert_kernel(split, ids_ref, own_ref, other_ref, w_in_ref, back_in_ref, back_out_ref, grad_own, grad_other, *kept_refs):
    x_ref, hid_ref, proj_ref, up_ref = kept_refs
    features, double = w_in_ref.shape
    hidden_units = double // 2
    size = own_ref.shape[0]
    w_in, back_in, back_out = w_in_ref[...], back_in_ref[...], back_out_ref[...]
    both = ((own_ref, grad_own), (other_ref, grad_other))
    start = 0
    for part in [[pair] for pair in both] if split else [both]:
        rows = size * len(part)
        lines = slice(start, start + rows)
        start += rows

        def taken(begin, end):
            return jnp.concatenate([ref[:, begin:end] for ref, _ in part], axis=0)

        x, upstream = taken(0, features), taken(features, 2 * features)
        gate = taken(2 * features, 2 * features + 1).astype(jnp.float32)
        projected = dot(x, w_in, (1, 0))
        back_raw = dot(upstream, back_out, (1, 0))
        gate_part, up_part = projected[:, :hidden_units], projected[:, hidden_units:]
        activated, derivative = silu_parts(gate_part)
        hidden = (activated * up_part).astype(jnp.bfloat16)
        score = jnp.sum(hidden.astype(jnp.float32) * back_raw, axis=1, keepdims=True)
        back_hidden = gate * back_raw
        grad_projected = jnp.concatenate(
            [back_hidden * up_part * derivative, back_hidden * activated], axis=1
        ).astype(jnp.bfloat16)
        x_ref[lines, :] = x
        hid_ref[lines, :] = hidden
        proj_ref[lines, :] = grad_projected
        up_ref[lines, :] = (gate * upstream.astype(jnp.float32)).astype(jnp.bfloat16)
        input_grad = dot(grad_projected, back_in, (1, 0)).astype(jnp.bfloat16)
        lane = lax.broadcasted_iota(jnp.int32, (rows, LANES), 1)
        scores = jnp.where(lane == ids_ref[0], score, 0.0).astype(jnp.bfloat16)
        for i, (_, out) in enumerate(part):
            out[:, :features] = input_grad[i * size : (i + 1) * size]
            out[:, features:] = scores[i * size : (i + 1) * size]


def transpose_kernel(*refs):
    for source, target in zip(refs[: len(refs) // 2], refs[len(refs) // 2 :]):
        target[...] = source[...].T


def spread_kernel(experts, rounds, own_ref, other_ref, *refs):
    count = len(refs) // 2
    chosen_refs, outs = refs[:count], refs[count:]
    for j in range(count):
        lines = slice(j * rounds, (j + 1) * rounds)
        chosen = chosen_refs[j][...]
        local, features = chosen.shape[1], outs[j].shape[1]
        grads = jnp.concatenate([own_ref[lines, :], other_ref[lines, :]], axis=0)
        outs[j][:local, :] = dot(chosen, grads[:, :features], (0, 0)).astype(jnp.bfloat16)
        scores = dot(grads[:, features:], chosen, (0, 0))[:experts]
        outs[j][local:, :] = fold(scores, features).astype(jnp.bfloat16)


def weights_kernel(begun, *refs):
    sums, groups, outs = refs[: 2 * begun], refs[2 * begun : -2], refs[-2:]
    for k, (left, right) in enumerate(((0, 2), (1, 3))):
        total = sums[k][...] if begun else None
        for g in range(0, len(groups), 4):
            part = dot(groups[g + left][...], groups[g + right][...], (0, 0))
            total = part if total is None else total + part
        if begun:
            outs[k][0] = total.astype(jnp.bfloat16)
        else:
            outs[k][...] = total


def call(kernel, outs, args, smem=0, hbm=0, scratch=(), dtype=jnp.bfloat16, flops=0, vmem=VMEM_LIMIT):
    in_specs = [pl.BlockSpec(memory_space=pltpu.SMEM)] * smem
    in_specs += [pl.BlockSpec(memory_space=pltpu.HBM)] * hbm
    in_specs += [pl.BlockSpec(memory_space=pltpu.VMEM)] * (len(args) - smem - hbm)
    return pl.pallas_call(
        kernel,
        out_shape=[jax.ShapeDtypeStruct(s, dtype) for s in outs],
        in_specs=in_specs,
        out_specs=[pl.BlockSpec(memory_space=pltpu.VMEM)] * len(outs),
        scratch_shapes=scratch,
        compiler_params=pltpu.CompilerParams(vmem_limit_bytes=vmem),
        cost_estimate=pl.CostEstimate(flops=flops, bytes_accessed=1 << 20, transcendentals=0),
    )(*args)


def ring_body(sizes, tokens, grad_out, routes, gates, w_gate_up, w_down):
    first_size, second_size = sizes
    local, features = tokens.shape
    top_count = routes.shape[1]
    experts = first_size * second_size
    per_round = experts // top_count
    rounds = local // per_round
    hidden_units = w_gate_up.shape[2] // 2
    ring = [(0, z) for z in range(second_size)] + [(1, z) for z in reversed(range(second_size))]
    length = len(ring)
    half = length // 2

    def device(place, core):
        x, z = ring[place % length]
        return (x * 2 + core) * second_size + z

    def shift(value, step):
        pairs = [(device(p, c), device(p + (step if c == 0 else -step), c)) for p in range(length) for c in range(2)]
        return lax.ppermute(value, AXES, pairs)

    def swap(value):
        pairs = [(device(p, c), device(p, 1 - c)) for p in range(length) for c in range(2)]
        return lax.ppermute(value, AXES, pairs)

    me, row = lax.axis_index("da"), lax.axis_index("db")
    core = lax.rem(me, 2)
    ids = jnp.stack([me * second_size + row, (me + 1 - 2 * core) * second_size + row]).astype(jnp.int32)

    (message,) = call(
        functools.partial(prepare_kernel, experts),
        [(2 * local + EXTRA, features)],
        [tokens, grad_out, routes.T, gates.T],
        hbm=4,
        vmem=WHOLE_VMEM,
        scratch=[
            pltpu.VMEM((top_count, local), routes.dtype),
            pltpu.VMEM((top_count, local), gates.dtype),
            pltpu.SemaphoreType.DMA((4,)),
        ],
    )
    mine, theirs = {0: message}, {}
    mine[1] = shift(mine[0], 1)
    theirs[0] = swap(mine[0])
    theirs[1] = shift(theirs[0], 1)

    def after(value, *earlier):
        return lax.optimization_barrier((value, *earlier))[0]

    w_in, w_out = w_gate_up[0], w_down[0]
    back_in, back_out = call(transpose_kernel, [w.shape[::-1] for w in (w_in, w_out)], [w_in, w_out])
    mine[1] = after(mine[1], back_in, back_out)
    own_sums, other_sums = {}, {}

    def pick(group, *earlier):
        size = len(group) * rounds
        shards = [(mine if own else theirs)[k] for own, k in group]
        if earlier:
            shards[-1] = after(shards[-1], *earlier)
        own, other, *chosen = call(
            functools.partial(select_kernel, experts, rounds, per_round),
            [(size, 2 * features + LANES)] * 2 + [(2 * rounds, local)] * len(group),
            [ids] + shards,
            smem=1,
            flops=8 * 4 * size * local * 2 * features,
        )
        return group, size, own, swap(other), chosen

    def work(picked):
        group, size, own, other, chosen = picked
        own_grad, other_grad, *kept = call(
            functools.partial(expert_kernel, size > LANES),
            [(size, features + LANES)] * 2
            + [(2 * size, n) for n in (features, hidden_units, 2 * hidden_units, features)],
            [ids, own, other, w_in, back_in, back_out],
            smem=1,
            flops=10 * 2 * 2 * size * features * 5 * hidden_units,
        )
        other_grad = swap(other_grad)
        spread = call(
            functools.partial(spread_kernel, experts, rounds),
            [(local + EXTRA, features)] * len(group),
            [own_grad, other_grad] + chosen,
            flops=8 * 4 * size * local * features,
        )
        for (own, k), total in zip(group, spread):
            (own_sums if own else other_sums)[k] = total
        return kept

    for k in range(1, half):
        mine[k + 1] = shift(mine[k], 1)
        if k + 1 < half:
            theirs[k + 1] = shift(theirs[k], 1)

    near = [[(True, 0), (True, 1), (False, 1)]] + [[(True, k), (False, k)] for k in range(2, half - 1)]
    kept = [array for group in near for array in work(pick(group))]
    done = [*own_sums.values(), *other_sums.values()]
    early = call(
        functools.partial(weights_kernel, False),
        [(features, 2 * hidden_units), (hidden_units, features)],
        kept,
        dtype=jnp.float32,
        flops=10 * 2 * sum(x.shape[0] for x in kept[::4]) * features * 3 * hidden_units,
    )
    kept = work(pick([(True, half - 1), (False, half - 1)]))
    kept = kept + work(pick([(True, half)], *done, kept[0]))

    def add(*terms):
        return sum(t.astype(jnp.float32) for t in terms).astype(jnp.bfloat16)

    there, here = other_sums[half - 1], own_sums[half - 1]
    far = shift(own_sums[half], -2)
    for k in range(half - 2, -1, -1):
        there, here = shift(there, -1), shift(here, -1)
        if k > 0:
            there = add(there, other_sums[k])
            here = add(here, own_sums[k], far) if k == half - 2 else add(here, own_sums[k])
    token_grads, gate_grads = call(
        functools.partial(finish_kernel, experts),
        [(local, features), (top_count, local)],
        [routes.T, own_sums[0], swap(there), here],
    )

    grad_in, grad_down = call(
        functools.partial(weights_kernel, True),
        [(1, features, 2 * hidden_units), (1, hidden_units, features)],
        list(early) + kept,
        smem=0,
        flops=10 * 2 * sum(x.shape[0] for x in kept[::4]) * features * 3 * hidden_units,
    )
    return token_grads, gate_grads.T, grad_in, grad_down


def solution(mesh):
    placed = (
        P(("groups", "replica", "da", "db"), None),
        P(("groups", "replica", "da", "db"), None),
        P(("groups", "replica", "da", "db"), None),
        P(("groups", "replica", "da", "db"), None),
        P(("da", "db"), "replica", None),
        P(("da", "db"), "replica", None),
    )
    first_size, second_size = mesh.shape["da"], mesh.shape["db"]
    experts = first_size * second_size

    def chosen_body(tokens, grad_out, routes, gates, w_gate_up, w_down):
        local, top_count = routes.shape
        dense = experts // top_count <= 2
        closed = mesh.shape["replica"] == 1 and first_size == 4 and second_size >= 3
        fits = local % LANES == 0 and experts % ROWS == 0 and experts <= LANES
        fits = fits and experts * local <= EXTRA * tokens.shape[1] and (local * top_count // experts) % ROWS == 0
        args = (tokens, grad_out, routes, gates, w_gate_up, w_down)
        if dense and closed and fits:
            return ring_body((first_size, second_size), *args)
        return body(*args)

    return jax.shard_map(
        chosen_body,
        mesh=mesh,
        in_specs=placed,
        out_specs=(
            P(("groups", "replica", "da", "db"), None),
            P(("groups", "replica", "da", "db"), None),
            P(("groups", "da", "db"), "replica", None),
            P(("groups", "da", "db"), "replica", None),
        ),
        check_vma=False,
    )
```
